32 devices in a mesh: seq: 8 (over z, y), ch: 4 (over x, core).
Axes of the slice: x: 2, y: 2, z: 4, core: 2. Of those that a mesh axis runs over, the one named last changes fastest.
Arguments:
- inputs: bfloat16 [512, 512, 1024], P('seq', None, 'ch'), may hold values from -6 to 6
- cotangent: bfloat16 [512, 512, 1024], P(None, 'seq', 'ch'), may hold values from -6 to 6
- right_weight: bfloat16 [512, 512], replicated, may hold values from -0.25 to 0.25
- left_weight: bfloat16 [512, 512], replicated, may hold values from -0.25 to 0.25
- first_gate: bfloat16 [512, 1024], P(None, 'ch'), may hold values from -4 to 4
- second_gate: bfloat16 [512, 1024], P(None, 'ch'), may hold values from -4 to 4
Outputs:
- output: bfloat16 [512, 512, 1024], P(None, 'seq', 'ch')
- grad_inputs: bfloat16 [512, 512, 1024], P('seq', None, 'ch')
- grad_right: float32 [512, 512], P(('seq', 'ch'))
- grad_left: float32 [512, 512], P(('seq', 'ch'))
- grad_first_gate: float32 [512, 1024], P('seq', 'ch')
- grad_second_gate: float32 [512, 1024], P('seq', 'ch')
The draws below stay inside these ranges and needn't reach their ends.
All inputs are finite; a program needn't handle non-finite values.
Results may differ from the reference program's by a relative error of at most 0.015.
Values may be sent and summed in bfloat16 or wider, within the bound.
No kernel may reach another device: no remote copies, remote signals or barrier semaphores. Data moves between devices by JAX's collectives and lax.ppermute only.
A program may use at most 256 MiB of HBM per device.

```python
import math
import jax
import jax.numpy as jnp
from jax import lax

GRID_ROWS = 512
GRID_COLS = 512
CHANNELS = 1024


def levels(stream_key, extent, cuts, smallest, high):
    level = 1.0
    for dim, parts in cuts:
        heights = jax.random.uniform(jax.random.fold_in(jax.random.fold_in(stream_key, 6), dim), (parts,), jnp.float32, smallest / len(cuts), high / len(cuts))
        level = level * jnp.repeat(jnp.exp(heights), extent[dim] // parts).reshape((-1,) + (1,) * (len(extent) - 1 - dim))
    return level


def bell_draw(stream_key, dims, deviation, limit, pieces=(), held_as=jnp.bfloat16):
    drawn = jax.random.normal(stream_key, dims, jnp.float32) * deviation
    if len(pieces) > 0:
        drawn = levels(stream_key, dims, pieces, -0.22, 0.18) * drawn
    return jnp.clip(drawn, min=-limit, max=limit).astype(held_as)


def setup_inputs(seed: int = 0) -> dict:
    key_of = jax.random.split(jax.random.key(seed), 7)
    return {
        "inputs": bell_draw(key_of[0], (GRID_ROWS, GRID_COLS, CHANNELS), 1.0, 6.0, ((0, 8), (2, 4))),
        "cotangent": bell_draw(key_of[1], (GRID_ROWS, GRID_COLS, CHANNELS), 1.0, 6.0, ((1, 8), (2, 4))),
        "right_weight": bell_draw(key_of[2], (GRID_COLS, GRID_COLS), GRID_COLS ** -0.5, 0.25),
        "left_weight": bell_draw(key_of[3], (GRID_ROWS, GRID_ROWS), GRID_ROWS ** -0.5, 0.25),
        "first_gate": bell_draw(key_of[4], (GRID_COLS, CHANNELS), 1.0, 4.0, ((1, 4),)),
        "second_gate": bell_draw(key_of[5], (GRID_ROWS, CHANNELS), 1.0, 4.0, ((1, 4),)),
    }


def block_pass(right32, left32, inputs, cotangent, first_gate, second_gate):
    section_one = jnp.einsum("kj,ijc->ikc", right32, inputs.astype(jnp.float32)).astype(jnp.bfloat16)
    gate_one = first_gate.astype(jnp.float32)[None, :, :]
    panels = (section_one.astype(jnp.float32) * gate_one).astype(jnp.bfloat16)
    mixed = jnp.einsum("mi,ikc->mkc", left32, panels.astype(jnp.float32))
    logistic = jax.nn.sigmoid(mixed)
    activated = mixed * logistic
    gate_two = second_gate.astype(jnp.float32)[:, None, :]
    output = (activated * gate_two).astype(jnp.bfloat16)
    grad_out = cotangent.astype(jnp.float32)
    grad_second = jnp.sum(grad_out * activated, axis=1)
    grad_mixed = (grad_out * gate_two * logistic * (1.0 + mixed * (1.0 - logistic))).astype(jnp.bfloat16)
    grad_left = jnp.einsum("mkc,ikc->mi", grad_mixed.astype(jnp.float32), panels.astype(jnp.float32))
    grad_panels = jnp.einsum("mi,mkc->ikc", left32, grad_mixed.astype(jnp.float32)).astype(jnp.bfloat16)
    grad_first = jnp.sum(grad_panels.astype(jnp.float32) * section_one.astype(jnp.float32), axis=0)
    grad_section = (grad_panels.astype(jnp.float32) * gate_one).astype(jnp.bfloat16)
    grad_inputs = jnp.einsum("kj,ikc->ijc", right32, grad_section.astype(jnp.float32)).astype(jnp.bfloat16)
    grad_right = jnp.einsum("ikc,ijc->kj", grad_section.astype(jnp.float32), inputs.astype(jnp.float32))
    return output, grad_inputs, grad_right, grad_left, grad_first, grad_second


def reference(inputs, cotangent, right_weight, left_weight, first_gate, second_gate):
    width = math.gcd(CHANNELS, 128)
    groups = CHANNELS // width
    right32 = right_weight.astype(jnp.float32)
    left32 = left_weight.astype(jnp.float32)

    def split(array):
        return jnp.moveaxis(array.reshape(array.shape[:-1] + (groups, width)), -2, 0)

    def joined(array):
        moved = jnp.moveaxis(array, 0, -2)
        return moved.reshape(moved.shape[:-2] + (CHANNELS,))

    def step(carry, blocks):
        output, grad_inputs, grad_right, grad_left, grad_first, grad_second = block_pass(right32, left32, blocks[0], blocks[1], blocks[2], blocks[3])
        return (carry[0] + grad_right, carry[1] + grad_left), (output, grad_inputs, grad_first, grad_second)

    start = (jnp.zeros((GRID_COLS, GRID_COLS), jnp.float32), jnp.zeros((GRID_ROWS, GRID_ROWS), jnp.float32))
    totals, stacked = lax.scan(step, start, (split(inputs), split(cotangent), split(first_gate), split(second_gate)))
    return (joined(stacked[0]), joined(stacked[1]), totals[0], totals[1], joined(stacked[2]), joined(stacked[3]))
```

```python
import functools

import jax
import jax.numpy as jnp
from jax import lax
from jax.experimental import pallas as pl
from jax.experimental.pallas import tpu as pltpu
from jax.sharding import PartitionSpec as P

BF16 = jnp.bfloat16
F32 = jnp.float32
LANES = 128
VMEM_LIMIT = 60 * 1024 * 1024


def section_kernel(blocks, w_ref, x_ref, out_ref):
    rows = x_ref.shape[0]
    w = w_ref[...]
    for first in range(0, rows, 2):
        pair = [x_ref[i] for i in range(first, min(first + 2, rows))]
        y = jnp.dot(w, jnp.concatenate(pair, axis=1), preferred_element_type=F32).astype(BF16)
        for p in range(len(pair)):
            part = y[:, p * LANES : (p + 1) * LANES]
            out_ref[:, first + p] = part.reshape(blocks, part.shape[0] // blocks, LANES)


def section_one(right, x, half, n):
    rows, cols, _ = x.shape
    step = min(8, rows)
    return pl.pallas_call(
        functools.partial(section_kernel, n),
        grid=(rows // step,),
        in_specs=[
            pl.BlockSpec((cols, cols), lambda i: (0, 0)),
            pl.BlockSpec((step, cols, LANES), lambda i: (i, 0, half)),
        ],
        out_specs=pl.BlockSpec((n, step, cols // n, LANES), lambda i: (0, i, 0, 0)),
        out_shape=jax.ShapeDtypeStruct((n, rows, cols // n, LANES), BF16),
        compiler_params=pltpu.CompilerParams(vmem_limit_bytes=VMEM_LIMIT),
        cost_estimate=pl.CostEstimate(
            flops=2 * rows * cols * cols * LANES,
            bytes_accessed=4 * rows * cols * LANES,
            transcendentals=0,
        ),
        name="section_one",
    )(right, x)


def joined(g_ref, i):
    block = g_ref[:, i]
    return block.reshape(block.shape[0] * block.shape[1], LANES)


def right_kernel(g_ref, x_ref, start_ref, out_ref, total):
    @pl.when(pl.program_id(0) == 0)
    def _():
        total[...] = start_ref[...]

    rows = x_ref.shape[0]
    g = jnp.concatenate([joined(g_ref, i) for i in range(rows)], axis=1)
    x = jnp.concatenate([x_ref[i] for i in range(rows)], axis=1)
    total[...] += lax.dot_general(g, x, (((1,), (1,)), ((), ())), preferred_element_type=F32)

    @pl.when(pl.program_id(0) == pl.num_programs(0) - 1)
    def _():
        out_ref[...] = total[...].astype(out_ref.dtype)


def grad_right_terms(g, x, half, start, dtype):
    n, rows, share, _ = g.shape
    cols = n * share
    step = min(8, rows)
    return pl.pallas_call(
        right_kernel,
        grid=(rows // step,),
        in_specs=[
            pl.BlockSpec((n, step, share, LANES), lambda i: (0, i, 0, 0)),
            pl.BlockSpec((step, cols, LANES), lambda i: (i, 0, half)),
            pl.BlockSpec((cols, cols), lambda i: (0, 0)),
        ],
        out_specs=pl.BlockSpec((cols, cols), lambda i: (0, 0)),
        out_shape=jax.ShapeDtypeStruct((cols, cols), dtype),
        scratch_shapes=[pltpu.VMEM((cols, cols), F32)],
        compiler_params=pltpu.CompilerParams(vmem_limit_bytes=VMEM_LIMIT),
        cost_estimate=pl.CostEstimate(
            flops=2 * rows * cols * cols * LANES,
            bytes_accessed=4 * rows * cols * LANES,
            transcendentals=0,
        ),
        name="grad_right",
    )(g, x, start)


def inputs_kernel(w_ref, g_ref, *refs):
    out_ref = refs[-1]
    rows = out_ref.shape[0]
    w = w_ref[...]
    for first in range(0, rows, 2):
        pair = [joined(g_ref, i) for i in range(first, min(first + 2, rows))]
        y = jnp.dot(w, jnp.concatenate(pair, axis=1), preferred_element_type=F32).astype(BF16)
        for p in range(len(pair)):
            out_ref[first + p] = y[:, p * LANES : (p + 1) * LANES]


def grad_inputs_half(right_t, g, half, channels, before):
    n, rows, share, _ = g.shape
    cols = n * share
    step = min(8, rows)
    in_specs = [
        pl.BlockSpec((cols, cols), lambda i: (0, 0)),
        pl.BlockSpec((n, step, share, LANES), lambda i: (0, i, 0, 0)),
    ]
    operands = [right_t, g]
    aliases = {}
    if before is not None:
        in_specs.append(pl.BlockSpec(memory_space=pl.ANY))
        operands.append(before)
        aliases = {2: 0}
    return pl.pallas_call(
        inputs_kernel,
        grid=(rows // step,),
        in_specs=in_specs,
        out_specs=pl.BlockSpec((step, cols, LANES), lambda i: (i, 0, half)),
        out_shape=jax.ShapeDtypeStruct((rows, cols, channels), BF16),
        input_output_aliases=aliases,
        compiler_params=pltpu.CompilerParams(vmem_limit_bytes=VMEM_LIMIT),
        cost_estimate=pl.CostEstimate(
            flops=2 * rows * cols * cols * LANES,
            bytes_accessed=4 * rows * cols * LANES,
            transcendentals=0,
        ),
        name="grad_inputs",
    )(*operands)


def place_kernel(part_ref, *refs):
    refs[-1][...] = part_ref[...]


def place_half(part, half, channels, before):
    rows, share, _ = part.shape
    step = min(64, rows)
    in_specs = [pl.BlockSpec((step, share, LANES), lambda i: (i, 0, 0))]
    operands = [part]
    aliases = {}
    if before is not None:
        in_specs.append(pl.BlockSpec(memory_space=pl.ANY))
        operands.append(before)
        aliases = {1: 0}
    return pl.pallas_call(
        place_kernel,
        grid=(rows // step,),
        in_specs=in_specs,
        out_specs=pl.BlockSpec((step, share, LANES), lambda i: (i, 0, half)),
        out_shape=jax.ShapeDtypeStruct((rows, share, channels), part.dtype),
        input_output_aliases=aliases,
        compiler_params=pltpu.CompilerParams(vmem_limit_bytes=VMEM_LIMIT),
        cost_estimate=pl.CostEstimate(
            flops=0, bytes_accessed=4 * rows * share * LANES, transcendentals=0
        ),
        name="place",
    )(*operands)


def scatter_sum(blocks, axis, size):
    if size & (size - 1):
        return lax.psum_scatter(blocks, axis, scatter_dimension=0)
    index = lax.axis_index(axis)
    bit = 1
    while bit < size:
        pairs = blocks.reshape((blocks.shape[0] // 2, 2) + blocks.shape[1:])
        mine = (index // bit) % 2
        kept = lax.dynamic_index_in_dim(pairs, mine, axis=1, keepdims=False)
        sent = lax.dynamic_index_in_dim(pairs, 1 - mine, axis=1, keepdims=False)
        blocks = kept + lax.ppermute(sent, axis, [(s, s ^ bit) for s in range(size)])
        bit *= 2
    return blocks[0]


def exchange(blocks):
    return lax.all_to_all(blocks, "seq", split_axis=0, concat_axis=0, tiled=True)


def middle(received, cotangent, left, gate_one, gate_two):
    n, rows, share, lanes = received.shape
    section = received.reshape(n * rows, share, lanes).astype(F32)
    gate_one = gate_one.astype(F32)[None]
    panels = (section * gate_one).astype(BF16)
    mixed = jnp.einsum("mi,ikd->mkd", left, panels, preferred_element_type=F32)
    logistic = jax.nn.sigmoid(mixed)
    activated = mixed * logistic
    gate_two = gate_two.astype(F32)[:, None, :]
    output = (activated * gate_two).astype(BF16)
    grad_out = cotangent.astype(F32)
    second = jnp.sum(grad_out * activated, axis=1)
    grad_mixed = (grad_out * gate_two * logistic * (1.0 + mixed * (1.0 - logistic))).astype(BF16)
    grad_left = jnp.einsum("mkd,ikd->mi", grad_mixed, panels, preferred_element_type=F32)
    grad_panels = jnp.einsum("mi,mkd->ikd", left, grad_mixed, preferred_element_type=F32)
    grad_panels = grad_panels.astype(BF16).astype(F32)
    first = jnp.sum(grad_panels * section, axis=0)
    grad_section = (grad_panels * gate_one).astype(BF16)
    return output, second, grad_left, first, grad_section.reshape(n, rows, share, lanes)


def per_device(sizes, inputs, cotangent, right_weight, left_weight, first_gate, second_gate):
    n, m = sizes
    rows, cols, channels = inputs.shape
    share = cols // n
    halves = channels // LANES
    mine = lax.dynamic_slice_in_dim(first_gate, lax.axis_index("seq") * share, share, axis=0)

    received = [exchange(section_one(right_weight, inputs, h, n)) for h in range(halves)]
    outs, seconds, lefts, firsts, returned = [], [], [], [], []
    for h in range(halves):
        lanes = slice(h * LANES, (h + 1) * LANES)
        output, second, left, first, grad_section = lax.optimization_barrier(
            middle(
                received[h],
                cotangent[:, :, lanes],
                left_weight,
                mine[:, lanes],
                second_gate[:, lanes],
            )
        )
        outs.append(output)
        seconds.append(second)
        lefts.append(left)
        firsts.append(first)
        returned.append(exchange(grad_section))

    grad_left = functools.reduce(jnp.add, lefts).reshape(n, m, -1, left_weight.shape[1])
    grad_left = scatter_sum(grad_left.swapaxes(0, 1), "ch", m)
    grad_second = jnp.concatenate(seconds, axis=1)
    both = jnp.concatenate([grad_left.reshape(n, -1), grad_second.reshape(n, -1)], axis=1)
    both = scatter_sum(both, "seq", n)
    size = grad_left.size // n
    grad_left = both[:size].reshape(-1, left_weight.shape[1])
    grad_second = both[size:].reshape(-1, channels)

    right_t = right_weight.T
    grad_first = jnp.concatenate(firsts, axis=1)
    output = None
    for h in range(halves):
        output = place_half(outs[h], h, channels, output)
    terms = jnp.zeros((cols, cols), F32)
    grad_inputs = None
    for h in range(halves - 1):
        terms = grad_right_terms(returned[h], inputs, h, terms, F32)
        grad_inputs = grad_inputs_half(right_t, returned[h], h, channels, grad_inputs)
    h = halves - 1
    returned[h], output, grad_first, terms, grad_inputs, right_t, grad_left, grad_second = (
        lax.optimization_barrier(
            (returned[h], output, grad_first, terms, grad_inputs, right_t, grad_left, grad_second)
        )
    )
    terms = grad_right_terms(returned[h], inputs, h, terms, BF16)
    terms = lax.all_to_all(
        terms.reshape(n * m, -1, cols), ("seq", "ch"), split_axis=0, concat_axis=0, tiled=True
    )
    grad_right = jnp.sum(terms.astype(F32), axis=0)
    grad_inputs = grad_inputs_half(right_t, returned[h], h, channels, grad_inputs)
    return output, grad_inputs, grad_right, grad_left, grad_first, grad_second


def solution(mesh):
    placed = (P("seq", None, "ch"), P(None, "seq", "ch"), P(), P(), P(None, "ch"), P(None, "ch"))
    return jax.shard_map(
        functools.partial(per_device, (mesh.shape["seq"], mesh.shape["ch"])),
        mesh=mesh,
        in_specs=placed,
        out_specs=(
            P(None, "seq", "ch"),
            P("seq", None, "ch"),
            P(("seq", "ch"), None),
            P(("seq", "ch"), None),
            P("seq", "ch"),
            P("seq", "ch"),
        ),
        check_vma=False,
    )
```

```python
import functools

import jax
import jax.numpy as jnp
from jax import lax
from jax.experimental import pallas as pl
from jax.experimental.pallas import tpu as pltpu
from jax.sharding import PartitionSpec as P

BF16 = jnp.bfloat16
F32 = jnp.float32
LANES = 128
VMEM_LIMIT = 60 * 1024 * 1024


def section_kernel(blocks, w_ref, x_ref, out_ref):
    rows = x_ref.shape[0]
    w = w_ref[...]
    for first in range(0, rows, 2):
        pair = [x_ref[i] for i in range(first, min(first + 2, rows))]
        y = jnp.dot(w, jnp.concatenate(pair, axis=1), preferred_element_type=F32).astype(BF16)
        for p in range(len(pair)):
            part = y[:, p * LANES : (p + 1) * LANES]
            out_ref[:, first + p] = part.reshape(blocks, part.shape[0] // blocks, LANES)


def section_one(right, x, half, n):
    rows, cols, _ = x.shape
    step = min(8, rows)
    return pl.pallas_call(
        functools.partial(section_kernel, n),
        grid=(rows // step,),
        in_specs=[
            pl.BlockSpec((cols, cols), lambda i: (0, 0)),
            pl.BlockSpec((step, cols, LANES), lambda i: (i, 0, half)),
        ],
        out_specs=pl.BlockSpec((n, step, cols // n, LANES), lambda i: (0, i, 0, 0)),
        out_shape=jax.ShapeDtypeStruct((n, rows, cols // n, LANES), BF16),
        compiler_params=pltpu.CompilerParams(vmem_limit_bytes=VMEM_LIMIT),
        cost_estimate=pl.CostEstimate(
            flops=2 * rows * cols * cols * LANES,
            bytes_accessed=4 * rows * cols * LANES,
            transcendentals=0,
        ),
        name="section_one",
    )(right, x)


def joined(g_ref, i):
    block = g_ref[:, i]
    return block.reshape(block.shape[0] * block.shape[1], LANES)


def right_kernel(g_ref, x_ref, start_ref, out_ref, total):
    @pl.when(pl.program_id(0) == 0)
    def _():
        total[...] = start_ref[...]

    rows = x_ref.shape[0]
    g = jnp.concatenate([joined(g_ref, i) for i in range(rows)], axis=1)
    x = jnp.concatenate([x_ref[i] for i in range(rows)], axis=1)
    total[...] += lax.dot_general(g, x, (((1,), (1,)), ((), ())), preferred_element_type=F32)

    @pl.when(pl.program_id(0) == pl.num_programs(0) - 1)
    def _():
        out_ref[...] = total[...].astype(out_ref.dtype)


def grad_right_terms(g, x, half, start, dtype):
    n, rows, share, _ = g.shape
    cols = n * share
    step = min(8, rows)
    return pl.pallas_call(
        right_kernel,
        grid=(rows // step,),
        in_specs=[
            pl.BlockSpec((n, step, share, LANES), lambda i: (0, i, 0, 0)),
            pl.BlockSpec((step, cols, LANES), lambda i: (i, 0, half)),
            pl.BlockSpec((cols, cols), lambda i: (0, 0)),
        ],
        out_specs=pl.BlockSpec((cols, cols), lambda i: (0, 0)),
        out_shape=jax.ShapeDtypeStruct((cols, cols), dtype),
        scratch_shapes=[pltpu.VMEM((cols, cols), F32)],
        compiler_params=pltpu.CompilerParams(vmem_limit_bytes=VMEM_LIMIT),
        cost_estimate=pl.CostEstimate(
            flops=2 * rows * cols * cols * LANES,
            bytes_accessed=4 * rows * cols * LANES,
            transcendentals=0,
        ),
        name="grad_right",
    )(g, x, start)


def inputs_kernel(w_ref, g_ref, *refs):
    out_ref = refs[-1]
    rows = out_ref.shape[0]
    w = w_ref[...]
    for first in range(0, rows, 2):
        pair = [joined(g_ref, i) for i in range(first, min(first + 2, rows))]
        y = jnp.dot(w, jnp.concatenate(pair, axis=1), preferred_element_type=F32).astype(BF16)
        for p in range(len(pair)):
            out_ref[first + p] = y[:, p * LANES : (p + 1) * LANES]


def grad_inputs_half(right_t, g, half, channels, before):
    n, rows, share, _ = g.shape
    cols = n * share
    step = min(8, rows)
    in_specs = [
        pl.BlockSpec((cols, cols), lambda i: (0, 0)),
        pl.BlockSpec((n, step, share, LANES), lambda i: (0, i, 0, 0)),
    ]
    operands = [right_t, g]
    aliases = {}
    if before is not None:
        in_specs.append(pl.BlockSpec(memory_space=pl.ANY))
        operands.append(before)
        aliases = {2: 0}
    return pl.pallas_call(
        inputs_kernel,
        grid=(rows // step,),
        in_specs=in_specs,
        out_specs=pl.BlockSpec((step, cols, LANES), lambda i: (i, 0, half)),
        out_shape=jax.ShapeDtypeStruct((rows, cols, channels), BF16),
        input_output_aliases=aliases,
        compiler_params=pltpu.CompilerParams(vmem_limit_bytes=VMEM_LIMIT),
        cost_estimate=pl.CostEstimate(
            flops=2 * rows * cols * cols * LANES,
            bytes_accessed=4 * rows * cols * LANES,
            transcendentals=0,
        ),
        name="grad_inputs",
    )(*operands)


def scatter_sum(blocks, axis, size, dtype):
    if size & (size - 1):
        return lax.psum_scatter(blocks, axis, scatter_dimension=0)
    index = lax.axis_index(axis)
    low = 1
    while low < size:
        radix = min(8, size // low)
        groups = blocks.reshape((blocks.shape[0] // radix, radix) + blocks.shape[1:])
        mine = (index // low) % radix
        blocks = lax.dynamic_index_in_dim(groups, mine, axis=1, keepdims=False)
        groups = groups.astype(dtype)
        for d in range(1, radix):
            sent = lax.dynamic_index_in_dim(groups, mine ^ d, axis=1, keepdims=False)
            pairs = [(s, s ^ (d * low)) for s in range(size)]
            blocks = blocks + lax.ppermute(sent, axis, pairs).astype(F32)
        low *= radix
    return blocks[0]


def exchange(blocks):
    return lax.all_to_all(blocks, "seq", split_axis=0, concat_axis=0, tiled=True)


def middle_kernel(
    left_ref, left_t_ref, s_ref, cot_ref, gate_one_ref, gate_two_ref, *refs
):
    out_ref, section_ref, terms_ref, first_ref, second_ref, terms, second = refs[-7:]
    group = pl.program_id(0)
    count = s_ref.shape[2]
    size = s_ref.shape[0] * s_ref.shape[1]
    part = min(8, count)

    @pl.when(group == 0)
    def _():
        terms[...] = jnp.zeros_like(terms)
        second[...] = jnp.zeros_like(second)

    def wide(value):
        return pltpu.einshape("akc->a(kc)", value)

    def deep(value):
        return pltpu.einshape("a(kc)->akc", value, k=part)

    gate_two = jnp.concatenate([gate_two_ref[...].astype(F32)] * part, axis=1)
    for k in range(0, count, part):
        near = slice(k, k + part)
        gate_one = gate_one_ref[near].astype(F32)
        gate_one = jnp.concatenate([gate_one[j : j + 1] for j in range(part)], axis=1)
        section = wide(s_ref[:, :, near].reshape(size, part, LANES)).astype(F32)
        panels = (section * gate_one).astype(BF16)
        mixed = jnp.dot(left_ref[...], panels, preferred_element_type=F32)
        logistic = 1.0 / (1.0 + jnp.exp(-mixed))
        activated = mixed * logistic
        out_ref[:, near] = deep((activated * gate_two).astype(BF16))
        cot = wide(cot_ref[:, near]).astype(F32)
        gated = cot * activated
        second[...] += sum(gated[:, j * LANES : (j + 1) * LANES] for j in range(part))
        grad = cot * gate_two * logistic * (1.0 + mixed * (1.0 - logistic))
        grad = grad.astype(BF16)
        terms[...] += lax.dot_general(
            grad, panels, (((1,), (1,)), ((), ())), preferred_element_type=F32
        )
        back = jnp.dot(left_t_ref[...], grad, preferred_element_type=F32).astype(BF16).astype(F32)
        sums = jnp.sum(back * section, axis=0, keepdims=True)
        for j in range(part):
            first_ref[k + j : k + j + 1, :] = sums[:, j * LANES : (j + 1) * LANES]
        back = deep((back * gate_one).astype(BF16))
        section_ref[:, :, near] = back.reshape(s_ref.shape[0], s_ref.shape[1], part, LANES)

    @pl.when(group == pl.num_programs(0) - 1)
    def _():
        terms_ref[...] = terms[...]
        second_ref[...] = second[...]


def middle(received, cotangent, left, left_t, gate_one, gate_two, half, before):
    n, rows, share, _ = received.shape
    size = n * rows
    step = min(16, share)
    in_specs = [
        pl.BlockSpec((size, size), lambda i: (0, 0)),
        pl.BlockSpec((size, size), lambda i: (0, 0)),
        pl.BlockSpec((n, rows, step, LANES), lambda i: (0, 0, i, 0)),
        pl.BlockSpec((size, step, LANES), lambda i: (0, i, half)),
        pl.BlockSpec((step, LANES), lambda i: (i, half)),
        pl.BlockSpec((size, LANES), lambda i: (0, half)),
    ]
    operands = [left, left_t, received, cotangent, gate_one, gate_two]
    aliases = {}
    if before is not None:
        in_specs.append(pl.BlockSpec(memory_space=pl.ANY))
        aliases = {len(operands): 0}
        operands.append(before)
    return pl.pallas_call(
        middle_kernel,
        grid=(share // step,),
        in_specs=in_specs,
        out_specs=[
            pl.BlockSpec((size, step, LANES), lambda i: (0, i, half)),
            pl.BlockSpec((n, rows, step, LANES), lambda i: (0, 0, i, 0)),
            pl.BlockSpec((size, size), lambda i: (0, 0)),
            pl.BlockSpec((step, LANES), lambda i: (i, 0)),
            pl.BlockSpec((size, LANES), lambda i: (0, 0)),
        ],
        out_shape=[
            jax.ShapeDtypeStruct(cotangent.shape, BF16),
            jax.ShapeDtypeStruct(received.shape, BF16),
            jax.ShapeDtypeStruct((size, size), F32),
            jax.ShapeDtypeStruct((share, LANES), F32),
            jax.ShapeDtypeStruct((size, LANES), F32),
        ],
        scratch_shapes=[pltpu.VMEM((size, size), F32), pltpu.VMEM((size, LANES), F32)],
        input_output_aliases=aliases,
        compiler_params=pltpu.CompilerParams(vmem_limit_bytes=VMEM_LIMIT),
        cost_estimate=pl.CostEstimate(
            flops=6 * size * size * share * LANES,
            bytes_accessed=8 * size * share * LANES,
            transcendentals=size * share * LANES,
        ),
        name="middle",
    )(*operands)


def per_device(sizes, inputs, cotangent, right_weight, left_weight, first_gate, second_gate):
    n, m = sizes
    rows, cols, channels = inputs.shape
    share = cols // n
    halves = channels // LANES
    mine = lax.dynamic_slice_in_dim(first_gate, lax.axis_index("seq") * share, share, axis=0)

    received = [exchange(section_one(right_weight, inputs, h, n)) for h in range(halves)]
    left_t = left_weight.T
    output = None
    seconds, lefts, firsts, returned = [], [], [], []
    for h in range(halves):
        output, grad_section, left, first, second = middle(
            received[h], cotangent, left_weight, left_t, mine, second_gate, h, output
        )
        seconds.append(second)
        lefts.append(left)
        firsts.append(first)
        returned.append(exchange(grad_section))

    grad_left = functools.reduce(jnp.add, lefts).reshape(n, m, -1, left_weight.shape[1])
    grad_left = scatter_sum(grad_left.swapaxes(0, 1), "ch", m, F32)
    grad_second = jnp.concatenate(seconds, axis=1)
    both = jnp.concatenate([grad_left.reshape(n, -1), grad_second.reshape(n, -1)], axis=1)
    both = scatter_sum(both, "seq", n, BF16)
    size = grad_left.size // n
    grad_left = both[:size].reshape(-1, left_weight.shape[1])
    grad_second = both[size:].reshape(-1, channels)

    right_t = right_weight.T
    grad_first = jnp.concatenate(firsts, axis=1)
    terms = jnp.zeros((cols, cols), F32)
    grad_inputs = None
    for h in range(halves - 1):
        terms = grad_right_terms(returned[h], inputs, h, terms, F32)
        grad_inputs = grad_inputs_half(right_t, returned[h], h, channels, grad_inputs)
    h = halves - 1
    returned[h], grad_first, terms, grad_inputs, right_t = lax.optimization_barrier(
        (returned[h], grad_first, terms, grad_inputs, right_t)
    )
    terms = grad_right_terms(returned[h], inputs, h, terms, BF16)
    terms = lax.all_to_all(
        terms.reshape(n * m, -1, cols), ("seq", "ch"), split_axis=0, concat_axis=0, tiled=True
    )
    grad_right = jnp.sum(terms.astype(F32), axis=0)
    grad_inputs = grad_inputs_half(right_t, returned[h], h, channels, grad_inputs)
    return output, grad_inputs, grad_right, grad_left, grad_first, grad_second


def solution(mesh):
    placed = (P("seq", None, "ch"), P(None, "seq", "ch"), P(), P(), P(None, "ch"), P(None, "ch"))
    return jax.shard_map(
        functools.partial(per_device, (mesh.shape["seq"], mesh.shape["ch"])),
        mesh=mesh,
        in_specs=placed,
        out_specs=(
            P(None, "seq", "ch"),
            P("seq", None, "ch"),
            P(("seq", "ch"), None),
            P(("seq", "ch"), None),
            P("seq", "ch"),
            P("seq", "ch"),
        ),
        check_vma=False,
    )
```

```python
import functools

import jax
import jax.numpy as jnp
from jax import lax
from jax.experimental import pallas as pl
from jax.experimental.pallas import tpu as pltpu
from jax.sharding import PartitionSpec as P

BF16 = jnp.bfloat16
F32 = jnp.float32
LANES = 128
VMEM_LIMIT = 60 * 1024 * 1024


def section_kernel(half, step, w_ref, x_ref, out_ref, x_buf, out_buf, in_sems, out_sems):
    blocks, rows, share, _ = out_buf.shape

    def fetch(c):
        near = pl.ds(c * step, step)
        lanes = pl.ds(half * LANES, LANES)
        return pltpu.make_async_copy(x_ref.at[near, :, lanes], x_buf.at[near], in_sems.at[c])

    def store(c):
        near = pl.ds(c * step, step)
        return pltpu.make_async_copy(out_buf.at[:, near], out_ref.at[:, near], out_sems.at[c])

    for c in range(rows // step):
        fetch(c).start()
    for c in range(rows // step):
        fetch(c).wait()
        group = jnp.concatenate([x_buf[c * step + i] for i in range(step)], axis=1)
        y = jnp.dot(w_ref[...], group, preferred_element_type=F32).astype(BF16)
        for i in range(step):
            part = y[:, i * LANES : (i + 1) * LANES]
            out_buf[:, c * step + i] = part.reshape(blocks, share, LANES)
        store(c).start()
    for c in range(rows // step):
        store(c).wait()


def section_one(right, x, half, n):
    rows, cols, _ = x.shape
    step = min(8, rows)
    count = rows // step
    return pl.pallas_call(
        functools.partial(section_kernel, half, step),
        in_specs=[
            pl.BlockSpec(memory_space=pltpu.VMEM),
            pl.BlockSpec(memory_space=pl.ANY),
        ],
        out_specs=pl.BlockSpec(memory_space=pl.ANY),
        out_shape=jax.ShapeDtypeStruct((n, rows, cols // n, LANES), BF16),
        scratch_shapes=[
            pltpu.VMEM((rows, cols, LANES), BF16),
            pltpu.VMEM((n, rows, cols // n, LANES), BF16),
            pltpu.SemaphoreType.DMA((count,)),
            pltpu.SemaphoreType.DMA((count,)),
        ],
        compiler_params=pltpu.CompilerParams(vmem_limit_bytes=VMEM_LIMIT),
        cost_estimate=pl.CostEstimate(
            flops=2 * rows * cols * cols * LANES,
            bytes_accessed=4 * rows * cols * LANES,
            transcendentals=0,
        ),
        name="section_one",
    )(right, x)


def joined(g_ref, i):
    block = g_ref[:, i]
    return block.reshape(block.shape[0] * block.shape[1], LANES)


def right_kernel(
    half, step, g_ref, x_ref, start_ref, out_ref, g_buf, x_buf, total, g_sems, x_sems
):
    rows = x_buf.shape[0]

    def fetch(c):
        near = pl.ds(c * step, step)
        lanes = pl.ds(half * LANES, LANES)
        return (
            pltpu.make_async_copy(g_ref.at[:, near], g_buf.at[:, near], g_sems.at[c]),
            pltpu.make_async_copy(x_ref.at[near, :, lanes], x_buf.at[near], x_sems.at[c]),
        )

    for c in range(rows // step):
        for copy in fetch(c):
            copy.start()
    total[...] = start_ref[...]
    for c in range(rows // step):
        for copy in fetch(c):
            copy.wait()
        near = range(c * step, (c + 1) * step)
        g = jnp.concatenate([joined(g_buf, i) for i in near], axis=1)
        x = jnp.concatenate([x_buf[i] for i in near], axis=1)
        total[...] += lax.dot_general(g, x, (((1,), (1,)), ((), ())), preferred_element_type=F32)
    out_ref[...] = total[...].astype(out_ref.dtype)


def grad_right_terms(g, x, half, start, dtype):
    n, rows, share, _ = g.shape
    cols = n * share
    step = min(8, rows)
    count = rows // step
    return pl.pallas_call(
        functools.partial(right_kernel, half, step),
        in_specs=[
            pl.BlockSpec(memory_space=pl.ANY),
            pl.BlockSpec(memory_space=pl.ANY),
            pl.BlockSpec(memory_space=pltpu.VMEM),
        ],
        out_specs=pl.BlockSpec(memory_space=pltpu.VMEM),
        out_shape=jax.ShapeDtypeStruct((cols, cols), dtype),
        scratch_shapes=[
            pltpu.VMEM((n, rows, share, LANES), BF16),
            pltpu.VMEM((rows, cols, LANES), BF16),
            pltpu.VMEM((cols, cols), F32),
            pltpu.SemaphoreType.DMA((count,)),
            pltpu.SemaphoreType.DMA((count,)),
        ],
        compiler_params=pltpu.CompilerParams(vmem_limit_bytes=VMEM_LIMIT),
        cost_estimate=pl.CostEstimate(
            flops=2 * rows * cols * cols * LANES,
            bytes_accessed=4 * rows * cols * LANES,
            transcendentals=0,
        ),
        name="grad_right",
    )(g, x, start)


def inputs_kernel(w_ref, g_ref, *refs):
    out_ref = refs[-1]
    rows = out_ref.shape[0]
    w = w_ref[...]
    for first in range(0, rows, 2):
        pair = [joined(g_ref, i) for i in range(first, min(first + 2, rows))]
        y = jnp.dot(w, jnp.concatenate(pair, axis=1), preferred_element_type=F32).astype(BF16)
        for p in range(len(pair)):
            out_ref[first + p] = y[:, p * LANES : (p + 1) * LANES]


def grad_inputs_half(right_t, g, half, channels, before):
    n, rows, share, _ = g.shape
    cols = n * share
    step = min(8, rows)
    in_specs = [
        pl.BlockSpec((cols, cols), lambda i: (0, 0)),
        pl.BlockSpec((n, step, share, LANES), lambda i: (0, i, 0, 0)),
    ]
    operands = [right_t, g]
    aliases = {}
    if before is not None:
        in_specs.append(pl.BlockSpec(memory_space=pl.ANY))
        operands.append(before)
        aliases = {2: 0}
    return pl.pallas_call(
        inputs_kernel,
        grid=(rows // step,),
        in_specs=in_specs,
        out_specs=pl.BlockSpec((step, cols, LANES), lambda i: (i, 0, half)),
        out_shape=jax.ShapeDtypeStruct((rows, cols, channels), BF16),
        input_output_aliases=aliases,
        compiler_params=pltpu.CompilerParams(vmem_limit_bytes=VMEM_LIMIT),
        cost_estimate=pl.CostEstimate(
            flops=2 * rows * cols * cols * LANES,
            bytes_accessed=4 * rows * cols * LANES,
            transcendentals=0,
        ),
        name="grad_inputs",
    )(*operands)


def scatter_sum(blocks, axis, size, dtype):
    if size & (size - 1):
        return lax.psum_scatter(blocks, axis, scatter_dimension=0)
    index = lax.axis_index(axis)
    low = 1
    while low < size:
        radix = min(8, size // low)
        groups = blocks.reshape((blocks.shape[0] // radix, radix) + blocks.shape[1:])
        mine = (index // low) % radix
        blocks = lax.dynamic_index_in_dim(groups, mine, axis=1, keepdims=False)
        groups = groups.astype(dtype)
        for d in range(1, radix):
            sent = lax.dynamic_index_in_dim(groups, mine ^ d, axis=1, keepdims=False)
            pairs = [(s, s ^ (d * low)) for s in range(size)]
            blocks = blocks + lax.ppermute(sent, axis, pairs).astype(F32)
        low *= radix
    return blocks[0]


def exchange(blocks, groups=None):
    return lax.all_to_all(
        blocks, "seq", split_axis=0, concat_axis=0, tiled=True, axis_index_groups=groups
    )


def middle_kernel(
    left_ref, left_t_ref, s_ref, cot_ref, gate_one_ref, gate_two_ref, *refs
):
    out_ref, section_ref, terms_ref, first_ref, second_ref, terms, second = refs[-7:]
    group = pl.program_id(0)
    count = s_ref.shape[2]
    size = s_ref.shape[0] * s_ref.shape[1]
    part = min(8, count)

    @pl.when(group == 0)
    def _():
        terms[...] = jnp.zeros_like(terms)
        second[...] = jnp.zeros_like(second)

    def wide(value):
        return pltpu.einshape("akc->a(kc)", value)

    def deep(value):
        return pltpu.einshape("a(kc)->akc", value, k=part)

    gate_two = jnp.concatenate([gate_two_ref[...].astype(F32)] * part, axis=1)
    for k in range(0, count, part):
        near = slice(k, k + part)
        gate_one = gate_one_ref[near].astype(F32)
        gate_one = jnp.concatenate([gate_one[j : j + 1] for j in range(part)], axis=1)
        section = wide(s_ref[:, :, near].reshape(size, part, LANES)).astype(F32)
        panels = (section * gate_one).astype(BF16)
        mixed = jnp.dot(left_ref[...], panels, preferred_element_type=F32)
        logistic = 1.0 / (1.0 + jnp.exp(-mixed))
        activated = mixed * logistic
        out_ref[:, near] = deep((activated * gate_two).astype(BF16))
        cot = wide(cot_ref[:, near]).astype(F32)
        gated = cot * activated
        second[...] += sum(gated[:, j * LANES : (j + 1) * LANES] for j in range(part))
        grad = cot * gate_two * logistic * (1.0 + mixed * (1.0 - logistic))
        grad = grad.astype(BF16)
        terms[...] += lax.dot_general(
            grad, panels, (((1,), (1,)), ((), ())), preferred_element_type=F32
        )
        back = jnp.dot(left_t_ref[...], grad, preferred_element_type=F32).astype(BF16).astype(F32)
        sums = jnp.sum(back * section, axis=0, keepdims=True)
        for j in range(part):
            first_ref[k + j : k + j + 1, :] = sums[:, j * LANES : (j + 1) * LANES]
        back = deep((back * gate_one).astype(BF16))
        section_ref[:, :, near] = back.reshape(s_ref.shape[0], s_ref.shape[1], part, LANES)

    @pl.when(group == pl.num_programs(0) - 1)
    def _():
        terms_ref[...] = terms[...]
        second_ref[...] = second[...]


def middle(received, cotangent, left, left_t, gate_one, gate_two, half, before):
    n, rows, share, _ = received.shape
    size = n * rows
    step = min(16, share)
    in_specs = [
        pl.BlockSpec((size, size), lambda i: (0, 0)),
        pl.BlockSpec((size, size), lambda i: (0, 0)),
        pl.BlockSpec((n, rows, step, LANES), lambda i: (0, 0, i, 0)),
        pl.BlockSpec((size, step, LANES), lambda i: (0, i, half)),
        pl.BlockSpec((step, LANES), lambda i: (i, half)),
        pl.BlockSpec((size, LANES), lambda i: (0, half)),
    ]
    operands = [left, left_t, received, cotangent, gate_one, gate_two]
    aliases = {}
    if before is not None:
        in_specs.append(pl.BlockSpec(memory_space=pl.ANY))
        aliases = {len(operands): 0}
        operands.append(before)
    return pl.pallas_call(
        middle_kernel,
        grid=(share // step,),
        in_specs=in_specs,
        out_specs=[
            pl.BlockSpec((size, step, LANES), lambda i: (0, i, half)),
            pl.BlockSpec((n, rows, step, LANES), lambda i: (0, 0, i, 0)),
            pl.BlockSpec((size, size), lambda i: (0, 0)),
            pl.BlockSpec((step, LANES), lambda i: (i, 0)),
            pl.BlockSpec((size, LANES), lambda i: (0, 0)),
        ],
        out_shape=[
            jax.ShapeDtypeStruct(cotangent.shape, BF16),
            jax.ShapeDtypeStruct(received.shape, BF16),
            jax.ShapeDtypeStruct((size, size), F32),
            jax.ShapeDtypeStruct((share, LANES), F32),
            jax.ShapeDtypeStruct((size, LANES), F32),
        ],
        scratch_shapes=[pltpu.VMEM((size, size), F32), pltpu.VMEM((size, LANES), F32)],
        input_output_aliases=aliases,
        compiler_params=pltpu.CompilerParams(vmem_limit_bytes=VMEM_LIMIT),
        cost_estimate=pl.CostEstimate(
            flops=6 * size * size * share * LANES,
            bytes_accessed=8 * size * share * LANES,
            transcendentals=size * share * LANES,
        ),
        name="middle",
    )(*operands)


def per_device(sizes, inputs, cotangent, right_weight, left_weight, first_gate, second_gate):
    n, m = sizes
    rows, cols, channels = inputs.shape
    share = cols // n
    halves = channels // LANES
    mine = lax.dynamic_slice_in_dim(first_gate, lax.axis_index("seq") * share, share, axis=0)

    received = [exchange(section_one(right_weight, inputs, h, n)) for h in range(halves)]
    left_t = left_weight.T
    output = None
    seconds, lefts, firsts, returned = [], [], [], []
    for h in range(halves):
        output, grad_section, left, first, second = middle(
            received[h], cotangent, left_weight, left_t, mine, second_gate, h, output
        )
        seconds.append(second)
        lefts.append(left)
        firsts.append(first)
        returned.append(exchange(grad_section))

    grad_left = functools.reduce(jnp.add, lefts).reshape(n, m, -1, left_weight.shape[1])
    grad_left = scatter_sum(grad_left.swapaxes(0, 1), "ch", m, F32)
    size = grad_left.size // n
    grad_second = jnp.concatenate(seconds, axis=1)
    both = jnp.concatenate([grad_left.reshape(n, -1), grad_second.reshape(n, -1)], axis=1)
    if n % 2 == 0:
        me = lax.axis_index("seq") % 2
        pairs = both.reshape(n // 2, 2, -1)
        sent = lax.dynamic_index_in_dim(pairs, 1 - me, axis=1, keepdims=False).astype(BF16)
        both = lax.dynamic_index_in_dim(pairs, me, axis=1, keepdims=False)
        both = both + lax.ppermute(sent, "seq", [(s, s ^ 1) for s in range(n)]).astype(F32)
        groups = [list(range(b, n, 2)) for b in range(2)]
    else:
        groups = None
    both = both.astype(BF16).reshape(both.shape[0], -1, LANES)

    right_t = right_weight.T
    grad_first = jnp.concatenate(firsts, axis=1)
    terms = jnp.zeros((cols, cols), F32)
    grad_inputs = None
    for h in range(halves - 1):
        terms = grad_right_terms(returned[h], inputs, h, terms, F32)
        grad_inputs = grad_inputs_half(right_t, returned[h], h, channels, grad_inputs)
    h = halves - 1
    returned[h], both, grad_first, terms, grad_inputs, right_t = lax.optimization_barrier(
        (returned[h], both, grad_first, terms, grad_inputs, right_t)
    )
    both = exchange(both, groups)
    both = jnp.sum(both.astype(F32), axis=0).reshape(-1)
    grad_left = both[:size].reshape(-1, left_weight.shape[1])
    grad_second = both[size:].reshape(-1, channels)
    terms = grad_right_terms(returned[h], inputs, h, terms, BF16)
    terms = lax.all_to_all(
        terms.reshape(n * m, -1, cols), ("seq", "ch"), split_axis=0, concat_axis=0, tiled=True
    )
    grad_right = jnp.sum(terms.astype(F32), axis=0)
    grad_inputs = grad_inputs_half(right_t, returned[h], h, channels, grad_inputs)
    return output, grad_inputs, grad_right, grad_left, grad_first, grad_second


def solution(mesh):
    placed = (P("seq", None, "ch"), P(None, "seq", "ch"), P(), P(), P(None, "ch"), P(None, "ch"))
    return jax.shard_map(
        functools.partial(per_device, (mesh.shape["seq"], mesh.shape["ch"])),
        mesh=mesh,
        in_specs=placed,
        out_specs=(
            P(None, "seq", "ch"),
            P("seq", None, "ch"),
            P(("seq", "ch"), None),
            P(("seq", "ch"), None),
            P("seq", "ch"),
            P("seq", "ch"),
        ),
        check_vma=False,
    )
```

```python
import functools

import jax
import jax.numpy as jnp
from jax import lax
from jax.experimental import pallas as pl
from jax.experimental.pallas import tpu as pltpu
from jax.sharding import PartitionSpec as P

BF16 = jnp.bfloat16
F32 = jnp.float32
LANES = 128
VMEM_LIMIT = 60 * 1024 * 1024


def section_kernel(half, step, w_ref, x_ref, out_ref, x_buf, out_buf, in_sems, out_sems):
    blocks, rows, share, _ = out_buf.shape

    def fetch(c):
        near = pl.ds(c * step, step)
        lanes = pl.ds(half * LANES, LANES)
        return pltpu.make_async_copy(x_ref.at[near, :, lanes], x_buf.at[near], in_sems.at[c])

    def store(c):
        near = pl.ds(c * step, step)
        return pltpu.make_async_copy(out_buf.at[:, near], out_ref.at[:, near], out_sems.at[c])

    for c in range(rows // step):
        fetch(c).start()
    for c in range(rows // step):
        fetch(c).wait()
        group = jnp.concatenate([x_buf[c * step + i] for i in range(step)], axis=1)
        y = jnp.dot(w_ref[...], group, preferred_element_type=F32).astype(BF16)
        for i in range(step):
            part = y[:, i * LANES : (i + 1) * LANES]
            out_buf[:, c * step + i] = part.reshape(blocks, share, LANES)
        store(c).start()
    for c in range(rows // step):
        store(c).wait()


def section_one(right, x, half, n):
    rows, cols, _ = x.shape
    step = min(8, rows)
    count = rows // step
    return pl.pallas_call(
        functools.partial(section_kernel, half, step),
        in_specs=[
            pl.BlockSpec(memory_space=pltpu.VMEM),
            pl.BlockSpec(memory_space=pl.ANY),
        ],
        out_specs=pl.BlockSpec(memory_space=pl.ANY),
        out_shape=jax.ShapeDtypeStruct((n, rows, cols // n, LANES), BF16),
        scratch_shapes=[
            pltpu.VMEM((rows, cols, LANES), BF16),
            pltpu.VMEM((n, rows, cols // n, LANES), BF16),
            pltpu.SemaphoreType.DMA((count,)),
            pltpu.SemaphoreType.DMA((count,)),
        ],
        compiler_params=pltpu.CompilerParams(vmem_limit_bytes=VMEM_LIMIT),
        cost_estimate=pl.CostEstimate(
            flops=2 * rows * cols * cols * LANES,
            bytes_accessed=4 * rows * cols * LANES,
            transcendentals=0,
        ),
        name="section_one",
    )(right, x)


def joined(g_ref, i):
    block = g_ref[:, i]
    return block.reshape(block.shape[0] * block.shape[1], LANES)


def right_kernel(
    half, step, g_ref, x_ref, start_ref, out_ref, g_buf, x_buf, total, g_sems, x_sems
):
    rows = x_buf.shape[0]

    def fetch(c):
        near = pl.ds(c * step, step)
        lanes = pl.ds(half * LANES, LANES)
        return (
            pltpu.make_async_copy(g_ref.at[:, near], g_buf.at[:, near], g_sems.at[c]),
            pltpu.make_async_copy(x_ref.at[near, :, lanes], x_buf.at[near], x_sems.at[c]),
        )

    for c in range(rows // step):
        for copy in fetch(c):
            copy.start()
    total[...] = start_ref[...]
    for c in range(rows // step):
        for copy in fetch(c):
            copy.wait()
        near = range(c * step, (c + 1) * step)
        g = jnp.concatenate([joined(g_buf, i) for i in near], axis=1)
        x = jnp.concatenate([x_buf[i] for i in near], axis=1)
        total[...] += lax.dot_general(g, x, (((1,), (1,)), ((), ())), preferred_element_type=F32)
    out_ref[...] = total[...].astype(out_ref.dtype)


def grad_right_terms(g, x, half, start, dtype):
    n, rows, share, _ = g.shape
    cols = n * share
    step = min(8, rows)
    count = rows // step
    return pl.pallas_call(
        functools.partial(right_kernel, half, step),
        in_specs=[
            pl.BlockSpec(memory_space=pl.ANY),
            pl.BlockSpec(memory_space=pl.ANY),
            pl.BlockSpec(memory_space=pltpu.VMEM),
        ],
        out_specs=pl.BlockSpec(memory_space=pltpu.VMEM),
        out_shape=jax.ShapeDtypeStruct((cols, cols), dtype),
        scratch_shapes=[
            pltpu.VMEM((n, rows, share, LANES), BF16),
            pltpu.VMEM((rows, cols, LANES), BF16),
            pltpu.VMEM((cols, cols), F32),
            pltpu.SemaphoreType.DMA((count,)),
            pltpu.SemaphoreType.DMA((count,)),
        ],
        compiler_params=pltpu.CompilerParams(vmem_limit_bytes=VMEM_LIMIT),
        cost_estimate=pl.CostEstimate(
            flops=2 * rows * cols * cols * LANES,
            bytes_accessed=4 * rows * cols * LANES,
            transcendentals=0,
        ),
        name="grad_right",
    )(g, x, start)


def inputs_kernel(w_ref, g_ref, *refs):
    out_ref = refs[-1]
    rows = out_ref.shape[0]
    w = w_ref[...]
    for first in range(0, rows, 2):
        pair = [joined(g_ref, i) for i in range(first, min(first + 2, rows))]
        y = jnp.dot(w, jnp.concatenate(pair, axis=1), preferred_element_type=F32).astype(BF16)
        for p in range(len(pair)):
            out_ref[first + p] = y[:, p * LANES : (p + 1) * LANES]


def grad_inputs_half(right_t, g, half, channels, before):
    n, rows, share, _ = g.shape
    cols = n * share
    step = min(8, rows)
    in_specs = [
        pl.BlockSpec((cols, cols), lambda i: (0, 0)),
        pl.BlockSpec((n, step, share, LANES), lambda i: (0, i, 0, 0)),
    ]
    operands = [right_t, g]
    aliases = {}
    if before is not None:
        in_specs.append(pl.BlockSpec(memory_space=pl.ANY))
        operands.append(before)
        aliases = {2: 0}
    return pl.pallas_call(
        inputs_kernel,
        grid=(rows // step,),
        in_specs=in_specs,
        out_specs=pl.BlockSpec((step, cols, LANES), lambda i: (i, 0, half)),
        out_shape=jax.ShapeDtypeStruct((rows, cols, channels), BF16),
        input_output_aliases=aliases,
        compiler_params=pltpu.CompilerParams(vmem_limit_bytes=VMEM_LIMIT),
        cost_estimate=pl.CostEstimate(
            flops=2 * rows * cols * cols * LANES,
            bytes_accessed=4 * rows * cols * LANES,
            transcendentals=0,
        ),
        name="grad_inputs",
    )(*operands)


def scatter_step(blocks, axis, size, low, radix, dtype):
    groups = blocks.reshape((blocks.shape[0] // radix, radix) + blocks.shape[1:])
    mine = (lax.axis_index(axis) // low) % radix
    blocks = lax.dynamic_index_in_dim(groups, mine, axis=1, keepdims=False)
    groups = groups.astype(dtype)
    for d in range(1, radix):
        sent = lax.dynamic_index_in_dim(groups, mine ^ d, axis=1, keepdims=False)
        pairs = [(s, s ^ (d * low)) for s in range(size)]
        blocks = blocks + lax.ppermute(sent, axis, pairs).astype(F32)
    return blocks


def scatter_sum(blocks, axis, size, dtype, low=1):
    if size & (size - 1):
        return lax.psum_scatter(blocks, axis, scatter_dimension=0)
    while low < size:
        radix = min(8, size // low)
        blocks = scatter_step(blocks, axis, size, low, radix, dtype)
        low *= radix
    return blocks[0]


def exchange(blocks):
    return lax.all_to_all(blocks, "seq", split_axis=0, concat_axis=0, tiled=True)


def middle_kernel(
    left_ref, left_t_ref, s_ref, cot_ref, gate_one_ref, gate_two_ref, *refs
):
    out_ref, section_ref, terms_ref, first_ref, second_ref, terms, second = refs[-7:]
    group = pl.program_id(0)
    count = s_ref.shape[2]
    size = s_ref.shape[0] * s_ref.shape[1]
    part = min(8, count)

    @pl.when(group == 0)
    def _():
        terms[...] = jnp.zeros_like(terms)
        second[...] = jnp.zeros_like(second)

    def wide(value):
        return pltpu.einshape("akc->a(kc)", value)

    def deep(value):
        return pltpu.einshape("a(kc)->akc", value, k=part)

    gate_two = jnp.concatenate([gate_two_ref[...].astype(F32)] * part, axis=1)
    for k in range(0, count, part):
        near = slice(k, k + part)
        gate_one = gate_one_ref[near].astype(F32)
        gate_one = jnp.concatenate([gate_one[j : j + 1] for j in range(part)], axis=1)
        section = wide(s_ref[:, :, near].reshape(size, part, LANES)).astype(F32)
        panels = (section * gate_one).astype(BF16)
        mixed = jnp.dot(left_ref[...], panels, preferred_element_type=F32)
        logistic = 1.0 / (1.0 + jnp.exp(-mixed))
        activated = mixed * logistic
        out_ref[:, near] = deep((activated * gate_two).astype(BF16))
        cot = wide(cot_ref[:, near]).astype(F32)
        gated = cot * activated
        second[...] += sum(gated[:, j * LANES : (j + 1) * LANES] for j in range(part))
        grad = cot * gate_two * logistic * (1.0 + mixed * (1.0 - logistic))
        grad = grad.astype(BF16)
        terms[...] += lax.dot_general(
            grad, panels, (((1,), (1,)), ((), ())), preferred_element_type=F32
        )
        back = jnp.dot(left_t_ref[...], grad, preferred_element_type=F32).astype(BF16).astype(F32)
        sums = jnp.sum(back * section, axis=0, keepdims=True)
        for j in range(part):
            first_ref[k + j : k + j + 1, :] = sums[:, j * LANES : (j + 1) * LANES]
        back = deep((back * gate_one).astype(BF16))
        section_ref[:, :, near] = back.reshape(s_ref.shape[0], s_ref.shape[1], part, LANES)

    @pl.when(group == pl.num_programs(0) - 1)
    def _():
        terms_ref[...] = terms[...]
        second_ref[...] = second[...]


def middle(received, cotangent, left, left_t, gate_one, gate_two, half, before):
    n, rows, share, _ = received.shape
    size = n * rows
    step = min(16, share)
    in_specs = [
        pl.BlockSpec((size, size), lambda i: (0, 0)),
        pl.BlockSpec((size, size), lambda i: (0, 0)),
        pl.BlockSpec((n, rows, step, LANES), lambda i: (0, 0, i, 0)),
        pl.BlockSpec((size, step, LANES), lambda i: (0, i, half)),
        pl.BlockSpec((step, LANES), lambda i: (i, half)),
        pl.BlockSpec((size, LANES), lambda i: (0, half)),
    ]
    operands = [left, left_t, received, cotangent, gate_one, gate_two]
    aliases = {}
    if before is not None:
        in_specs.append(pl.BlockSpec(memory_space=pl.ANY))
        aliases = {len(operands): 0}
        operands.append(before)
    return pl.pallas_call(
        middle_kernel,
        grid=(share // step,),
        in_specs=in_specs,
        out_specs=[
            pl.BlockSpec((size, step, LANES), lambda i: (0, i, half)),
            pl.BlockSpec((n, rows, step, LANES), lambda i: (0, 0, i, 0)),
            pl.BlockSpec((size, size), lambda i: (0, 0)),
            pl.BlockSpec((step, LANES), lambda i: (i, 0)),
            pl.BlockSpec((size, LANES), lambda i: (0, 0)),
        ],
        out_shape=[
            jax.ShapeDtypeStruct(cotangent.shape, BF16),
            jax.ShapeDtypeStruct(received.shape, BF16),
            jax.ShapeDtypeStruct((size, size), F32),
            jax.ShapeDtypeStruct((share, LANES), F32),
            jax.ShapeDtypeStruct((size, LANES), F32),
        ],
        scratch_shapes=[pltpu.VMEM((size, size), F32), pltpu.VMEM((size, LANES), F32)],
        input_output_aliases=aliases,
        compiler_params=pltpu.CompilerParams(vmem_limit_bytes=VMEM_LIMIT),
        cost_estimate=pl.CostEstimate(
            flops=6 * size * size * share * LANES,
            bytes_accessed=8 * size * share * LANES,
            transcendentals=size * share * LANES,
        ),
        name="middle",
    )(*operands)


def per_device(sizes, inputs, cotangent, right_weight, left_weight, first_gate, second_gate):
    n, m = sizes
    rows, cols, channels = inputs.shape
    share = cols // n
    halves = channels // LANES
    mine = lax.dynamic_slice_in_dim(first_gate, lax.axis_index("seq") * share, share, axis=0)

    received = [exchange(section_one(right_weight, inputs, h, n)) for h in range(halves)]
    left_t = left_weight.T
    output = None
    seconds, lefts, firsts, returned = [], [], [], []
    for h in range(halves):
        output, grad_section, left, first, second = middle(
            received[h], cotangent, left_weight, left_t, mine, second_gate, h, output
        )
        seconds.append(second)
        lefts.append(left)
        firsts.append(first)
        returned.append(exchange(grad_section))

    grad_left = functools.reduce(jnp.add, lefts).reshape(n, m, -1, left_weight.shape[1])
    grad_left = scatter_sum(grad_left.swapaxes(0, 1), "ch", m, F32)
    size = grad_left.size // n
    grad_second = jnp.concatenate(seconds, axis=1)
    both = jnp.concatenate([grad_left.reshape(n, -1), grad_second.reshape(n, -1)], axis=1)
    low = 1
    if n > 2 and n & (n - 1) == 0:
        both = scatter_step(both, "seq", n, 1, 2, BF16)
        low = 2

    right_t = right_weight.T
    grad_first = jnp.concatenate(firsts, axis=1)
    terms = jnp.zeros((cols, cols), F32)
    grad_inputs = None
    for h in range(halves - 1):
        terms = grad_right_terms(returned[h], inputs, h, terms, F32)
        grad_inputs = grad_inputs_half(right_t, returned[h], h, channels, grad_inputs)
    h = halves - 1
    returned[h], grad_first, terms, grad_inputs, right_t = lax.optimization_barrier(
        (returned[h], grad_first, terms, grad_inputs, right_t)
    )
    terms = grad_right_terms(returned[h], inputs, h, terms, BF16)
    terms, both = lax.optimization_barrier((terms, both))
    terms = lax.all_to_all(
        terms.reshape(n * m, -1, cols), ("seq", "ch"), split_axis=0, concat_axis=0, tiled=True
    )
    grad_right = jnp.sum(terms.astype(F32), axis=0)
    both = scatter_sum(both, "seq", n, BF16, low)
    grad_left = both[:size].reshape(-1, left_weight.shape[1])
    grad_second = both[size:].reshape(-1, channels)
    grad_inputs = grad_inputs_half(right_t, returned[h], h, channels, grad_inputs)
    return output, grad_inputs, grad_right, grad_left, grad_first, grad_second


def solution(mesh):
    placed = (P("seq", None, "ch"), P(None, "seq", "ch"), P(), P(), P(None, "ch"), P(None, "ch"))
    return jax.shard_map(
        functools.partial(per_device, (mesh.shape["seq"], mesh.shape["ch"])),
        mesh=mesh,
        in_specs=placed,
        out_specs=(
            P(None, "seq", "ch"),
            P("seq", None, "ch"),
            P(("seq", "ch"), None),
            P(("seq", "ch"), None),
            P("seq", "ch"),
            P("seq", "ch"),
        ),
        check_vma=False,
    )
```

```python
import functools

import jax
import jax.numpy as jnp
from jax import lax
from jax.experimental import pallas as pl
from jax.experimental.pallas import tpu as pltpu
from jax.sharding import PartitionSpec as P

BF16 = jnp.bfloat16
F32 = jnp.float32
LANES = 128
VMEM_LIMIT = 60 * 1024 * 1024


def section_kernel(half, step, w_ref, x_ref, out_ref, x_buf, out_buf, in_sems, out_sems):
    blocks, rows, share, _ = out_buf.shape

    def fetch(c):
        near = pl.ds(c * step, step)
        lanes = pl.ds(half * LANES, LANES)
        return pltpu.make_async_copy(x_ref.at[near, :, lanes], x_buf.at[near], in_sems.at[c])

    def store(c):
        near = pl.ds(c * step, step)
        return pltpu.make_async_copy(out_buf.at[:, near], out_ref.at[:, near], out_sems.at[c])

    for c in range(rows // step):
        fetch(c).start()
    for c in range(rows // step):
        fetch(c).wait()
        group = jnp.concatenate([x_buf[c * step + i] for i in range(step)], axis=1)
        y = jnp.dot(w_ref[...], group, preferred_element_type=F32).astype(BF16)
        for i in range(step):
            part = y[:, i * LANES : (i + 1) * LANES]
            out_buf[:, c * step + i] = part.reshape(blocks, share, LANES)
        store(c).start()
    for c in range(rows // step):
        store(c).wait()


def section_one(right, x, half, n):
    rows, cols, _ = x.shape
    step = min(8, rows)
    count = rows // step
    return pl.pallas_call(
        functools.partial(section_kernel, half, step),
        in_specs=[
            pl.BlockSpec(memory_space=pltpu.VMEM),
            pl.BlockSpec(memory_space=pl.ANY),
        ],
        out_specs=pl.BlockSpec(memory_space=pl.ANY),
        out_shape=jax.ShapeDtypeStruct((n, rows, cols // n, LANES), BF16),
        scratch_shapes=[
            pltpu.VMEM((rows, cols, LANES), BF16),
            pltpu.VMEM((n, rows, cols // n, LANES), BF16),
            pltpu.SemaphoreType.DMA((count,)),
            pltpu.SemaphoreType.DMA((count,)),
        ],
        compiler_params=pltpu.CompilerParams(vmem_limit_bytes=VMEM_LIMIT),
        cost_estimate=pl.CostEstimate(
            flops=2 * rows * cols * cols * LANES,
            bytes_accessed=4 * rows * cols * LANES,
            transcendentals=0,
        ),
        name="section_one",
    )(right, x)


def joined(g_ref, i):
    block = g_ref[:, i]
    return block.reshape(block.shape[0] * block.shape[1], LANES)


def right_kernel(
    half, step, g_ref, x_ref, start_ref, out_ref, g_buf, x_buf, total, g_sems, x_sems
):
    rows = x_buf.shape[0]

    def fetch(c):
        near = pl.ds(c * step, step)
        lanes = pl.ds(half * LANES, LANES)
        return (
            pltpu.make_async_copy(g_ref.at[:, near], g_buf.at[:, near], g_sems.at[c]),
            pltpu.make_async_copy(x_ref.at[near, :, lanes], x_buf.at[near], x_sems.at[c]),
        )

    for c in range(rows // step):
        for copy in fetch(c):
            copy.start()
    total[...] = start_ref[...]
    for c in range(rows // step):
        for copy in fetch(c):
            copy.wait()
        near = range(c * step, (c + 1) * step)
        g = jnp.concatenate([joined(g_buf, i) for i in near], axis=1)
        x = jnp.concatenate([x_buf[i] for i in near], axis=1)
        total[...] += lax.dot_general(g, x, (((1,), (1,)), ((), ())), preferred_element_type=F32)
    out_ref[...] = total[...].astype(out_ref.dtype)


def grad_right_terms(g, x, half, start, dtype):
    n, rows, share, _ = g.shape
    cols = n * share
    step = min(8, rows)
    count = rows // step
    return pl.pallas_call(
        functools.partial(right_kernel, half, step),
        in_specs=[
            pl.BlockSpec(memory_space=pl.ANY),
            pl.BlockSpec(memory_space=pl.ANY),
            pl.BlockSpec(memory_space=pltpu.VMEM),
        ],
        out_specs=pl.BlockSpec(memory_space=pltpu.VMEM),
        out_shape=jax.ShapeDtypeStruct((cols, cols), dtype),
        scratch_shapes=[
            pltpu.VMEM((n, rows, share, LANES), BF16),
            pltpu.VMEM((rows, cols, LANES), BF16),
            pltpu.VMEM((cols, cols), F32),
            pltpu.SemaphoreType.DMA((count,)),
            pltpu.SemaphoreType.DMA((count,)),
        ],
        compiler_params=pltpu.CompilerParams(vmem_limit_bytes=VMEM_LIMIT),
        cost_estimate=pl.CostEstimate(
            flops=2 * rows * cols * cols * LANES,
            bytes_accessed=4 * rows * cols * LANES,
            transcendentals=0,
        ),
        name="grad_right",
    )(g, x, start)


def inputs_kernel(w_ref, g_ref, *refs):
    out_ref = refs[-1]
    rows = out_ref.shape[0]
    w = w_ref[...]
    for first in range(0, rows, 2):
        pair = [joined(g_ref, i) for i in range(first, min(first + 2, rows))]
        y = jnp.dot(w, jnp.concatenate(pair, axis=1), preferred_element_type=F32).astype(BF16)
        for p in range(len(pair)):
            out_ref[first + p] = y[:, p * LANES : (p + 1) * LANES]


def grad_inputs_half(right_t, g, half, channels, before, piece=0, pieces=1):
    n, rows, share, _ = g.shape
    cols = n * share
    step = min(8, rows)
    count = rows // step // pieces
    skip = piece * count
    in_specs = [
        pl.BlockSpec((cols, cols), lambda i: (0, 0)),
        pl.BlockSpec((n, step, share, LANES), lambda i: (0, i + skip, 0, 0)),
    ]
    operands = [right_t, g]
    aliases = {}
    if before is not None:
        in_specs.append(pl.BlockSpec(memory_space=pl.ANY))
        operands.append(before)
        aliases = {2: 0}
    return pl.pallas_call(
        inputs_kernel,
        grid=(count,),
        in_specs=in_specs,
        out_specs=pl.BlockSpec((step, cols, LANES), lambda i: (i + skip, 0, half)),
        out_shape=jax.ShapeDtypeStruct((rows, cols, channels), BF16),
        input_output_aliases=aliases,
        compiler_params=pltpu.CompilerParams(vmem_limit_bytes=VMEM_LIMIT),
        cost_estimate=pl.CostEstimate(
            flops=2 * count * step * cols * cols * LANES,
            bytes_accessed=4 * count * step * cols * LANES,
            transcendentals=0,
        ),
        name="grad_inputs",
    )(*operands)


def scatter_step(blocks, axis, size, low, radix, dtype):
    groups = blocks.reshape((blocks.shape[0] // radix, radix) + blocks.shape[1:])
    mine = (lax.axis_index(axis) // low) % radix
    blocks = lax.dynamic_index_in_dim(groups, mine, axis=1, keepdims=False)
    groups = groups.astype(dtype)
    for d in range(1, radix):
        sent = lax.dynamic_index_in_dim(groups, mine ^ d, axis=1, keepdims=False)
        pairs = [(s, s ^ (d * low)) for s in range(size)]
        blocks = blocks + lax.ppermute(sent, axis, pairs).astype(F32)
    return blocks


def scatter_sum(blocks, axis, size, dtype, low=1):
    if size & (size - 1):
        return lax.psum_scatter(blocks, axis, scatter_dimension=0)
    while low < size:
        radix = min(8, size // low)
        blocks = scatter_step(blocks, axis, size, low, radix, dtype)
        low *= radix
    return blocks[0]


def exchange(blocks):
    return lax.all_to_all(blocks, "seq", split_axis=0, concat_axis=0, tiled=True)


def middle_kernel(
    left_ref, left_t_ref, s_ref, cot_ref, gate_one_ref, gate_two_ref, *refs
):
    out_ref, section_ref, terms_ref, first_ref, second_ref, terms, second = refs[-7:]
    group = pl.program_id(0)
    count = s_ref.shape[2]
    size = s_ref.shape[0] * s_ref.shape[1]
    part = min(8, count)

    @pl.when(group == 0)
    def _():
        terms[...] = jnp.zeros_like(terms)
        second[...] = jnp.zeros_like(second)

    def wide(value):
        return pltpu.einshape("akc->a(kc)", value)

    def deep(value):
        return pltpu.einshape("a(kc)->akc", value, k=part)

    gate_two = jnp.concatenate([gate_two_ref[...].astype(F32)] * part, axis=1)
    for k in range(0, count, part):
        near = slice(k, k + part)
        gate_one = gate_one_ref[near].astype(F32)
        gate_one = jnp.concatenate([gate_one[j : j + 1] for j in range(part)], axis=1)
        section = wide(s_ref[:, :, near].reshape(size, part, LANES)).astype(F32)
        panels = (section * gate_one).astype(BF16)
        mixed = jnp.dot(left_ref[...], panels, preferred_element_type=F32)
        logistic = 1.0 / (1.0 + jnp.exp(-mixed))
        activated = mixed * logistic
        out_ref[:, near] = deep((activated * gate_two).astype(BF16))
        cot = wide(cot_ref[:, near]).astype(F32)
        gated = cot * activated
        second[...] += sum(gated[:, j * LANES : (j + 1) * LANES] for j in range(part))
        grad = cot * gate_two * logistic * (1.0 + mixed * (1.0 - logistic))
        grad = grad.astype(BF16)
        terms[...] += lax.dot_general(
            grad, panels, (((1,), (1,)), ((), ())), preferred_element_type=F32
        )
        back = jnp.dot(left_t_ref[...], grad, preferred_element_type=F32).astype(BF16).astype(F32)
        sums = jnp.sum(back * section, axis=0, keepdims=True)
        for j in range(part):
            first_ref[k + j : k + j + 1, :] = sums[:, j * LANES : (j + 1) * LANES]
        back = deep((back * gate_one).astype(BF16))
        section_ref[:, :, near] = back.reshape(s_ref.shape[0], s_ref.shape[1], part, LANES)

    @pl.when(group == pl.num_programs(0) - 1)
    def _():
        terms_ref[...] = terms[...]
        second_ref[...] = second[...]


def middle(received, cotangent, left, left_t, gate_one, gate_two, half, before):
    n, rows, share, _ = received.shape
    size = n * rows
    step = min(16, share)
    in_specs = [
        pl.BlockSpec((size, size), lambda i: (0, 0)),
        pl.BlockSpec((size, size), lambda i: (0, 0)),
        pl.BlockSpec((n, rows, step, LANES), lambda i: (0, 0, i, 0)),
        pl.BlockSpec((size, step, LANES), lambda i: (0, i, half)),
        pl.BlockSpec((step, LANES), lambda i: (i, half)),
        pl.BlockSpec((size, LANES), lambda i: (0, half)),
    ]
    operands = [left, left_t, received, cotangent, gate_one, gate_two]
    aliases = {}
    if before is not None:
        in_specs.append(pl.BlockSpec(memory_space=pl.ANY))
        aliases = {len(operands): 0}
        operands.append(before)
    return pl.pallas_call(
        middle_kernel,
        grid=(share // step,),
        in_specs=in_specs,
        out_specs=[
            pl.BlockSpec((size, step, LANES), lambda i: (0, i, half)),
            pl.BlockSpec((n, rows, step, LANES), lambda i: (0, 0, i, 0)),
            pl.BlockSpec((size, size), lambda i: (0, 0)),
            pl.BlockSpec((step, LANES), lambda i: (i, 0)),
            pl.BlockSpec((size, LANES), lambda i: (0, 0)),
        ],
        out_shape=[
            jax.ShapeDtypeStruct(cotangent.shape, BF16),
            jax.ShapeDtypeStruct(received.shape, BF16),
            jax.ShapeDtypeStruct((size, size), F32),
            jax.ShapeDtypeStruct((share, LANES), F32),
            jax.ShapeDtypeStruct((size, LANES), F32),
        ],
        scratch_shapes=[pltpu.VMEM((size, size), F32), pltpu.VMEM((size, LANES), F32)],
        input_output_aliases=aliases,
        compiler_params=pltpu.CompilerParams(vmem_limit_bytes=VMEM_LIMIT),
        cost_estimate=pl.CostEstimate(
            flops=6 * size * size * share * LANES,
            bytes_accessed=8 * size * share * LANES,
            transcendentals=size * share * LANES,
        ),
        name="middle",
    )(*operands)


def per_device(sizes, inputs, cotangent, right_weight, left_weight, first_gate, second_gate):
    n, m = sizes
    rows, cols, channels = inputs.shape
    share = cols // n
    halves = channels // LANES
    mine = lax.dynamic_slice_in_dim(first_gate, lax.axis_index("seq") * share, share, axis=0)

    received = [exchange(section_one(right_weight, inputs, h, n)) for h in range(halves)]
    left_t = left_weight.T
    output = None
    seconds, lefts, firsts, returned = [], [], [], []
    for h in range(halves):
        output, grad_section, left, first, second = middle(
            received[h], cotangent, left_weight, left_t, mine, second_gate, h, output
        )
        seconds.append(second)
        lefts.append(left)
        firsts.append(first)
        returned.append(exchange(grad_section))

    grad_left = functools.reduce(jnp.add, lefts).reshape(n, m, -1, left_weight.shape[1])
    grad_left = scatter_sum(grad_left.swapaxes(0, 1), "ch", m, F32)
    size = grad_left.size // n
    grad_second = jnp.concatenate(seconds, axis=1)
    both = jnp.concatenate([grad_left.reshape(n, -1), grad_second.reshape(n, -1)], axis=1)
    low = 1
    if n > 2 and n & (n - 1) == 0:
        both = scatter_step(both, "seq", n, 1, 2, BF16)
        low = 2

    right_t = right_weight.T
    grad_first = jnp.concatenate(firsts, axis=1)
    terms = jnp.zeros((cols, cols), F32)
    grad_inputs = None
    for h in range(halves - 1):
        terms = grad_right_terms(returned[h], inputs, h, terms, F32)
        grad_inputs = grad_inputs_half(right_t, returned[h], h, channels, grad_inputs)
    h = halves - 1
    returned[h], grad_first, terms, grad_inputs, right_t = lax.optimization_barrier(
        (returned[h], grad_first, terms, grad_inputs, right_t)
    )
    terms = grad_right_terms(returned[h], inputs, h, terms, BF16)
    terms, returned[h] = lax.optimization_barrier((terms, returned[h]))
    terms = lax.all_to_all(
        terms.reshape(n * m, -1, cols), ("seq", "ch"), split_axis=0, concat_axis=0, tiled=True
    )
    grad_right = jnp.sum(terms.astype(F32), axis=0)
    pieces = 2 if rows % 16 == 0 else 1
    for piece in range(pieces):
        grad_inputs = grad_inputs_half(
            right_t, returned[h], h, channels, grad_inputs, piece, pieces
        )
        if piece == 0:
            grad_inputs, both = lax.optimization_barrier((grad_inputs, both))
            both = scatter_sum(both, "seq", n, BF16, low)
    grad_left = both[:size].reshape(-1, left_weight.shape[1])
    grad_second = both[size:].reshape(-1, channels)
    return output, grad_inputs, grad_right, grad_left, grad_first, grad_second


def solution(mesh):
    placed = (P("seq", None, "ch"), P(None, "seq", "ch"), P(), P(), P(None, "ch"), P(None, "ch"))
    return jax.shard_map(
        functools.partial(per_device, (mesh.shape["seq"], mesh.shape["ch"])),
        mesh=mesh,
        in_specs=placed,
        out_specs=(
            P(None, "seq", "ch"),
            P("seq", None, "ch"),
            P(("seq", "ch"), None),
            P(("seq", "ch"), None),
            P("seq", "ch"),
            P("seq", "ch"),
        ),
        check_vma=False,
    )
```
